32 devices in a mesh: frame: 8 (over z, x), chan: 4 (over y, core).
Axes of the slice: x: 2, y: 2, z: 4, core: 2. Of those that a mesh axis runs over, the one named last changes fastest.
Arguments:
- query_act: bfloat16 [7040, 2240], P('frame', 'chan'), may hold values from -6 to 6
- key_act: bfloat16 [7040, 2240], P('frame', 'chan'), may hold values from -6 to 6
- value_act: bfloat16 [7040, 2240], P('frame', 'chan'), may hold values from -6 to 6
- conv_weight: bfloat16 [3, 2240, 2240], P(None, 'chan'), may hold values from -0.109375 to 0.109375
- gate_act: bfloat16 [7040, 2240], P('frame', 'chan'), may hold values from -8 to 8
Outputs:
- layer_out: bfloat16 [7040, 2240], P('frame', 'chan')
The draws below stay inside these ranges and needn't reach their ends.
All inputs are finite; a program needn't handle non-finite values.
Results may differ from the reference program's by a relative error of at most 0.015.
Values may be sent and summed in bfloat16 or wider, within the bound.
A program may use at most 128 MiB of HBM per device.

```python
import jax
import jax.numpy as jnp
from jax import lax

D = 2240
HEADS = 20
HD = 112
TPF = 880
TOKENS = 7040
N_CHAN = 4


def raised(array, key, source, target, shards_of, factor):
    owner, partner = [(jnp.arange(array.shape[axis_at]) // (array.shape[axis_at] // shards_of)).reshape([-1 if axis == axis_at else 1 for axis in range(array.ndim)]) for axis_at in (source, target)]
    chosen = jax.random.permutation(key, shards_of)[partner]
    strong = (owner == chosen) | (owner == (partner + shards_of // 2) % shards_of)
    return jnp.where(strong, factor * array, array)


def block_levels(rng, extent, pieces, smallest, largest):
    factor_of, own = 1.0, jax.random.fold_in(rng, 6)
    for position, parts in pieces:
        draws = jnp.exp(jax.random.uniform(jax.random.fold_in(own, position), (parts,), jnp.float32, smallest / len(pieces), largest / len(pieces)))
        factor_of = factor_of * jnp.repeat(draws, extent[position] // parts).reshape([-1 if axis == position else 1 for axis in range(len(extent))])
    return factor_of


def noise(own_key, extent, width, limit, cuts=(), kind=jnp.bfloat16):
    result = width * jax.random.normal(own_key, extent, jnp.float32)
    if cuts:
        result = result * block_levels(own_key, extent, cuts, -0.22, 0.18)
    return jnp.clip(result, -limit, limit).astype(kind)


def gaussian_with(stream_key, shape, scale, most, pieces, heavy, dtype=jnp.bfloat16):
    drawn = scale * jax.random.normal(stream_key, shape, jnp.float32)
    if pieces:
        drawn = drawn * block_levels(stream_key, shape, pieces, -0.22, 0.18)
    return jnp.clip(raised(drawn, jax.random.fold_in(stream_key, 3), *heavy), -most, most).astype(dtype)


def setup_inputs(seed: int = 0) -> dict:
    splits = jax.random.split(jax.random.key(seed), 6)
    return {
        "query_act": noise(splits[0], (TOKENS, D), 1.0, 6.0, ((0, 8), (1, 4))),
        "key_act": noise(splits[1], (TOKENS, D), 1.0, 6.0, ((0, 8), (1, 4))),
        "value_act": noise(splits[2], (TOKENS, D), 1.0, 6.0, ((0, 8), (1, 4))),
        "conv_weight": gaussian_with(splits[3], (3, D, D), (3 * D) ** -0.5, 0.109375, ((1, 4),), (1, 2, 4, 2.0)),
        "gate_act": noise(splits[4], (TOKENS, D), 1.5, 8.0, ((0, 8), (1, 4))),
    }


def reference(query_act, key_act, value_act, conv_weight, gate_act):
    frame_count = TOKENS // TPF
    key_feat = jnp.maximum(key_act, 0).astype(jnp.float32).reshape(frame_count, TPF, HEADS, HD)
    value_feat = value_act.astype(jnp.float32).reshape(frame_count, TPF, HEADS, HD)
    query_feat = jnp.maximum(query_act, 0).astype(jnp.float32).reshape(frame_count, TPF, HEADS, HD)
    frame_state = jnp.einsum('ftha,fthb->fhab', key_feat, value_feat)
    prefix_state = jnp.cumsum(frame_state, axis=0).astype(jnp.bfloat16)
    prefix_state = lax.optimization_barrier(prefix_state).astype(jnp.float32)
    readout = jnp.einsum('ftha,fhab->fthb', query_feat, prefix_state)
    scale_inv = lax.rsqrt(lax.optimization_barrier(jnp.mean(readout * readout, axis=-1, keepdims=True)) + 1e-06)
    attended = (readout * scale_inv).astype(jnp.bfloat16).reshape(frame_count, TPF, D)
    with_rims = jnp.pad(attended, ((1, 1), (0, 0), (0, 0)))
    group_width = D // N_CHAN
    conv_out = jnp.zeros((frame_count * TPF, D), jnp.float32)
    for chan_group in range(N_CHAN):
        low_col = chan_group * group_width
        partials = jnp.zeros((frame_count * TPF, D), jnp.float32)
        for tap_index in range(3):
            source = with_rims[tap_index:tap_index + frame_count, :, low_col:low_col + group_width]
            partials = partials + jnp.dot(source.reshape(frame_count * TPF, group_width), conv_weight[tap_index, low_col:low_col + group_width, :], preferred_element_type=jnp.float32)
        rounded = lax.optimization_barrier(partials.astype(jnp.bfloat16))
        conv_out = conv_out + rounded.astype(jnp.float32)
    gate_value = jax.nn.silu(gate_act.astype(jnp.float32))
    return (conv_out * gate_value).astype(jnp.bfloat16)
```

```python
import functools

import jax
import jax.numpy as jnp
from jax import lax
from jax.experimental import pallas as pl
from jax.experimental.pallas import tpu as pltpu
from jax.sharding import PartitionSpec as P

HD = 112
TPF = 880
PARTS = 2
F32 = jnp.float32
BF16 = jnp.bfloat16
MESH = pl.DeviceIdType.MESH


def kernel(
    frames,
    q_ref, k_ref, v_ref, w_hbm, g_hbm, out_ref,
    w_all, wb, wsib, gate, own_state, pair_state, chain_in, chain_out, spread, qx,
    a_own, a_sib, cross, cross_in, kept, back, back_in,
    load_sem, w_send, w_recv, x_send, x_recv, c_send, c_recv, q_send, q_recv,
    s_send, s_recv, h_send, h_recv, f_send, f_recv, y_send, y_recv, b_send, b_recv,
):
    rows, width = q_ref.shape
    half = qx.shape[0]
    chunk = half // PARTS
    shift = rows - half
    heads = width // HD
    pairs = frames // 2
    f = lax.axis_index("frame")
    m = lax.axis_index("chan")
    x = lax.rem(f, 2)
    p = f // 2
    first, last = p == 0, p == pairs - 1
    sib_m = m + 1 - 2 * lax.rem(m, 2)
    far_m = m + 2 - 4 * lax.rem(m // 2, 2)
    far_sib_m = far_m + 1 - 2 * lax.rem(far_m, 2)
    sib, far, mate = (f, sib_m), (f, far_m), (f + 1 - 2 * x, m)
    up, down = (f - 2, m), (f + 2, m)

    def remote(src, dst, send, recv, device):
        return pltpu.make_async_remote_copy(
            src_ref=src, dst_ref=dst, send_sem=send, recv_sem=recv,
            device_id=device, device_id_type=MESH,
        )

    taps = w_hbm.shape[0]
    loads = [pltpu.make_async_copy(w_hbm.at[t], w_all.at[t], load_sem.at[t]) for t in range(taps)]
    loads.append(pltpu.make_async_copy(g_hbm, gate, load_sem.at[taps]))
    for load in loads:
        load.start()

    barrier = pltpu.get_barrier_semaphore()
    for device in (sib, far, mate):
        pl.semaphore_signal(barrier, inc=1, device_id=device, device_id_type=MESH)

    @pl.when(jnp.logical_not(first))
    def _():
        pl.semaphore_signal(barrier, inc=1, device_id=up, device_id_type=MESH)

    @pl.when(jnp.logical_not(last))
    def _():
        pl.semaphore_signal(barrier, inc=1, device_id=down, device_id_type=MESH)

    col_head = lax.broadcasted_iota(jnp.int32, (HD, width), 1) // HD
    full = lax.dot_general(
        jnp.maximum(k_ref[...], 0), v_ref[...], (((0,), (0,)), ((), ())),
        preferred_element_type=F32,
    )
    state = jnp.zeros((HD, width), F32)
    for h in range(heads):
        state = jnp.where(col_head == h, full[h * HD:(h + 1) * HD, :], state)
    own_state[...] = state.astype(BF16)

    pl.semaphore_wait(barrier, 3 + jnp.where(first, 0, 1) + jnp.where(last, 0, 1))

    swap = remote(own_state, pair_state, x_send.at[0], x_recv.at[0], mate)
    swap.start()
    mate_row = pl.multiple_of((1 - x) * shift, 16)
    q_moves = [
        remote(
            q_ref.at[pl.ds(pl.multiple_of(mate_row + i * chunk, 16), chunk), :],
            qx.at[pl.ds(i * chunk, chunk), :], q_send.at[i], q_recv.at[i], mate,
        )
        for i in range(PARTS)
    ]
    for move in q_moves:
        move.start()

    for t in range(taps):
        loads[t].wait()
        for b in range(wb.shape[0]):
            wb[b, t] = w_all[t, :, b * width:(b + 1) * width]
    w_moves = [
        remote(wb.at[far_sib_m], wsib.at[1], w_send.at[0], w_recv.at[0], sib),
        remote(wb.at[sib_m], wsib.at[0], w_send.at[1], w_recv.at[1], sib),
    ]
    for move in w_moves:
        move.start()

    @pl.when(first)
    def _():
        a_own[0] = jnp.zeros((half, width), BF16)
        a_sib[0] = jnp.zeros((half, width), BF16)
        chain_in[...] = jnp.zeros((HD, width), BF16)

    @pl.when(last)
    def _():
        a_own[3] = jnp.zeros((half, width), BF16)
        a_sib[3] = jnp.zeros((half, width), BF16)

    swap.wait()
    cuts = [(0, 64), (64, HD - 64)]
    chain = [
        remote(
            chain_out.at[pl.ds(at, size), :], chain_in.at[pl.ds(at, size), :],
            c_send.at[i], c_recv.at[i], down,
        )
        for i, (at, size) in enumerate(cuts)
    ]
    for i, (at, size) in enumerate(cuts):
        @pl.when(jnp.logical_not(first))
        def _():
            chain[i].wait_recv()

        span = pl.ds(at, size)
        before = chain_in[span, :].astype(F32)
        mine = own_state[span, :].astype(F32)
        other = pair_state[span, :].astype(F32)
        low = jnp.where(x == 0, mine, other)
        chain_out[span, :] = (before + mine + other).astype(BF16)

        @pl.when(jnp.logical_not(last))
        def _():
            chain[i].start()

        own_state[span, :] = (before + low).astype(BF16)

    for j, source in enumerate((own_state, chain_out)):
        for h in range(heads):
            spread[j, h * HD:(h + 1) * HD, :] = jnp.where(col_head == h, source[...], 0)

    lanes = 128
    group = (
        lax.broadcasted_iota(jnp.int32, (width, lanes), 0) // HD
        == lax.broadcasted_iota(jnp.int32, (width, lanes), 1)
    ).astype(BF16)
    ungroup = (
        lax.broadcasted_iota(jnp.int32, (lanes, width), 1) // HD
        == lax.broadcasted_iota(jnp.int32, (lanes, width), 0)
    ).astype(BF16)

    def attend(query, prefix):
        readout = jnp.dot(jnp.maximum(query, 0), prefix, preferred_element_type=F32)
        total = jnp.dot((readout * readout).astype(BF16), group, preferred_element_type=F32)
        inverse = lax.rsqrt(total * (1.0 / HD) + 1e-06)
        coarse = inverse.astype(BF16)
        fine = (inverse - coarse.astype(F32)).astype(BF16)
        factor = jnp.dot(coarse, ungroup, preferred_element_type=F32)
        factor = factor + jnp.dot(fine, ungroup, preferred_element_type=F32)
        return (readout * factor).astype(BF16)

    def part(ref, slot, i):
        return ref.at[slot, pl.ds(pl.multiple_of(i * chunk, 16), chunk), :]

    def to_sib(slot, i):
        return remote(part(a_own, slot, i), part(a_sib, slot, i), s_send.at[slot - 1, i], s_recv.at[slot - 1, i], sib)

    def go_down(i):
        return remote(part(a_own, 2, i), part(a_own, 0, i), h_send.at[0, i], h_recv.at[0, i], down)

    def go_up(i):
        return remote(part(a_own, 1, i), part(a_own, 3, i), h_send.at[1, i], h_recv.at[1, i], up)

    def forward(j, i):
        return remote(part(a_own, 3 * j, i), part(a_sib, 3 * j, i), f_send.at[j, i], f_recv.at[j, i], sib)

    my_row = pl.multiple_of(x * shift, 16)
    for i in range(PARTS):
        span = pl.ds(i * chunk, chunk)
        mine = attend(q_ref[pl.ds(pl.multiple_of(my_row + i * chunk, 16), chunk), :], spread[x])
        a_own[1 + x, span, :] = mine
        q_moves[i].wait_recv()
        a_own[2 - x, span, :] = attend(qx[span, :], spread[1 - x])

        @pl.when(jnp.logical_not(last))
        def _():
            go_down(i).start()

        @pl.when(jnp.logical_not(first))
        def _():
            go_up(i).start()

        to_sib(1, i).start()
        to_sib(2, i).start()

    def y_move(s):
        return remote(cross.at[s], cross_in.at[s], y_send.at[s], y_recv.at[s], far)

    def b_move(i):
        return remote(back.at[i], back_in.at[i], b_send.at[i], b_recv.at[i], mate)

    def gated(total, at):
        span = pl.ds(pl.multiple_of(at, 16), chunk)
        u = gate[span, :].astype(F32)
        out_ref[span, :] = (total * (u / (1.0 + jnp.exp(-u)))).astype(BF16)

    def finish(s):
        j, i = s // PARTS, lax.rem(s, PARTS)
        y_move(s).wait_recv()
        total = kept[s] + cross_in[s].astype(F32)

        @pl.when(j == x)
        def _():
            gated(total, my_row + i * chunk)

        @pl.when(j != x)
        def _():
            back[i] = total.astype(BF16)
            b_move(i).start()

    loads[taps].wait()
    w_moves[0].wait_recv()
    w_moves[1].wait_recv()

    def step(s, carry):
        j, i = s // PARTS, lax.rem(s, PARTS)
        span = pl.ds(pl.multiple_of(i * chunk, 16), chunk)

        @pl.when(j == 0)
        def _():
            to_sib(1, i).wait_recv()
            to_sib(2, i).wait_recv()

        def dot(a, slot, w):
            return jnp.dot(a[slot, span, :], w[...], preferred_element_type=F32)

        def inner(mine, theirs):
            acc = dot(a_own, 1, mine.at[1 - j]) + dot(a_own, 2, mine.at[2 - j])
            return acc + dot(a_sib, 1, theirs.at[1 - j]) + dot(a_sib, 2, theirs.at[2 - j])

        def outer(mine, theirs):
            return dot(a_own, 3 * j, mine.at[2 * j]) + dot(a_sib, 3 * j, theirs.at[2 * j])

        has = jnp.logical_and(p + j > 0, p + j < pairs)

        @pl.when(has)
        def _():
            remote(part(a_own, 2 - j, i), part(a_own, 3 * j, i), h_send.at[j, i], h_recv.at[j, i], sib).wait_recv()
            forward(j, i).start()

        kept[s] = inner(wb.at[far_m], wsib.at[1])

        @pl.when(has)
        def _():
            forward(j, i).wait_recv()

        cross[s] = (kept[s] + outer(wb.at[far_m], wsib.at[1])).astype(BF16)
        y_move(s).start()
        kept[s] = inner(wb.at[m], wsib.at[0]) + outer(wb.at[m], wsib.at[0])

        @pl.when(s > 0)
        def _():
            finish(s - 1)

        return carry

    steps = 2 * PARTS
    lax.fori_loop(0, steps, step, 0)
    finish(steps - 1)
    for i in range(PARTS):
        b_move(i).wait_recv()
        gated(back_in[i].astype(F32), mate_row + i * chunk)

    for move in q_moves:
        move.wait_send()
    for move in w_moves:
        move.wait_send()
    for s in range(steps):
        y_move(s).wait_send()

    for i in range(PARTS):
        to_sib(1, i).wait_send()
        to_sib(2, i).wait_send()
        b_move(i).wait_send()

        @pl.when(jnp.logical_not(last))
        def _():
            go_down(i).wait_send()
            forward(1, i).wait_send()

        @pl.when(jnp.logical_not(first))
        def _():
            go_up(i).wait_send()
            forward(0, i).wait_send()

    @pl.when(jnp.logical_not(last))
    def _():
        for move in chain:
            move.wait_send()


def shards(frames, query_act, key_act, value_act, conv_weight, gate_act):
    rows, width = query_act.shape
    taps, _, outs = conv_weight.shape
    chans = outs // width
    assert rows == TPF and frames % 2 == 0 and chans == 4
    half = -(-rows // (32 * PARTS)) * 16 * PARTS
    chunk = half // PARTS
    dma = pltpu.SemaphoreType.DMA
    vmem = pl.BlockSpec(memory_space=pltpu.VMEM)
    hbm = pl.BlockSpec(memory_space=pl.ANY)
    return pl.pallas_call(
        functools.partial(kernel, frames),
        out_shape=jax.ShapeDtypeStruct((rows, width), BF16),
        in_specs=[vmem, vmem, vmem, hbm, hbm],
        out_specs=vmem,
        scratch_shapes=[
            pltpu.VMEM((taps, width, outs), BF16),
            pltpu.VMEM((chans, taps, width, width), BF16),
            pltpu.VMEM((2, taps, width, width), BF16),
            pltpu.VMEM((rows, width), BF16),
            pltpu.VMEM((HD, width), BF16),
            pltpu.VMEM((HD, width), BF16),
            pltpu.VMEM((HD, width), BF16),
            pltpu.VMEM((HD, width), BF16),
            pltpu.VMEM((2, width, width), BF16),
            pltpu.VMEM((half, width), BF16),
            pltpu.VMEM((4, half, width), BF16),
            pltpu.VMEM((4, half, width), BF16),
            pltpu.VMEM((2 * PARTS, chunk, width), BF16),
            pltpu.VMEM((2 * PARTS, chunk, width), BF16),
            pltpu.VMEM((2 * PARTS, chunk, width), F32),
            pltpu.VMEM((PARTS, chunk, width), BF16),
            pltpu.VMEM((PARTS, chunk, width), BF16),
            dma((taps + 1,)),
            dma((2,)), dma((2,)),
            dma((1,)), dma((1,)),
            dma((2,)), dma((2,)),
            dma((PARTS,)), dma((PARTS,)),
            dma((2, PARTS)), dma((2, PARTS)),
            dma((2, PARTS)), dma((2, PARTS)),
            dma((2, PARTS)), dma((2, PARTS)),
            dma((2 * PARTS,)), dma((2 * PARTS,)),
            dma((PARTS,)), dma((PARTS,)),
        ],
        compiler_params=pltpu.CompilerParams(
            collective_id=0, has_side_effects=True, vmem_limit_bytes=56 * 1024 * 1024
        ),
    )(query_act, key_act, value_act, conv_weight, gate_act)


def solution(mesh):
    return jax.shard_map(
        functools.partial(shards, mesh.shape["frame"]),
        mesh=mesh,
        in_specs=(
            P("frame", "chan"),
            P("frame", "chan"),
            P("frame", "chan"),
            P(None, "chan", None),
            P("frame", "chan"),
        ),
        out_specs=P("frame", "chan"),
        check_vma=False,
    )
```

```python
import functools

import jax
import jax.numpy as jnp
from jax import lax
from jax.experimental import pallas as pl
from jax.experimental.pallas import tpu as pltpu
from jax.sharding import PartitionSpec as P

HD = 112
TPF = 880
PARTS = 4
F32 = jnp.float32
BF16 = jnp.bfloat16
MESH = pl.DeviceIdType.MESH


def kernel(
    frames,
    q_hbm, k_hbm, v_hbm, w_hbm, g_hbm, out_ref,
    turned, q_ref, w_all, wb, wsib, gate, own_state, pair_state, chain_in, chain_out, spread, qx,
    a_own, a_sib, cross, cross_in, kept, back, back_in,
    load_sem, w_send, w_recv, x_send, x_recv, c_send, c_recv, q_send, q_recv,
    s_send, s_recv, h_send, h_recv, f_send, f_recv, y_send, y_recv, b_send, b_recv,
):
    rows, width = q_ref.shape
    half = qx.shape[0]
    chunk = half // PARTS
    shift = rows - half
    heads = width // HD
    pairs = frames // 2
    f = lax.axis_index("frame")
    m = lax.axis_index("chan")
    x = lax.rem(f, 2)
    p = f // 2
    first, last = p == 0, p == pairs - 1
    sib_m = m + 1 - 2 * lax.rem(m, 2)
    far_m = m + 2 - 4 * lax.rem(m // 2, 2)
    far_sib_m = far_m + 1 - 2 * lax.rem(far_m, 2)
    sib, far, mate = (f, sib_m), (f, far_m), (f + 1 - 2 * x, m)
    up, down = (f - 2, m), (f + 2, m)

    def remote(src, dst, send, recv, device):
        return pltpu.make_async_remote_copy(
            src_ref=src, dst_ref=dst, send_sem=send, recv_sem=recv,
            device_id=device, device_id_type=MESH,
        )

    barrier = pltpu.get_barrier_semaphore()
    for device in (sib, far, mate):
        pl.semaphore_signal(barrier, inc=1, device_id=device, device_id_type=MESH)

    @pl.when(jnp.logical_not(first))
    def _():
        pl.semaphore_signal(barrier, inc=1, device_id=up, device_id_type=MESH)

    @pl.when(jnp.logical_not(last))
    def _():
        pl.semaphore_signal(barrier, inc=1, device_id=down, device_id_type=MESH)

    taps = w_hbm.shape[0]
    moves = [
        pltpu.make_async_copy(source, turned.at[i], load_sem.at[taps + i])
        for i, source in enumerate((q_hbm, k_hbm, v_hbm, g_hbm))
    ]
    loads = [pltpu.make_async_copy(w_hbm.at[t], w_all.at[t], load_sem.at[t]) for t in range(taps)]
    for load in moves + loads:
        load.start()

    moves[0].wait()
    q_ref[...] = jnp.transpose(turned[0])
    pl.semaphore_wait(barrier, 3 + jnp.where(first, 0, 1) + jnp.where(last, 0, 1))
    mate_row = pl.multiple_of((1 - x) * shift, 16)
    q_moves = [
        remote(
            q_ref.at[pl.ds(pl.multiple_of(mate_row + i * chunk, 16), chunk), :],
            qx.at[pl.ds(i * chunk, chunk), :], q_send.at[i], q_recv.at[i], mate,
        )
        for i in range(PARTS)
    ]
    q_moves[0].start()

    col_head = lax.broadcasted_iota(jnp.int32, (HD, width), 1) // HD
    moves[1].wait()
    moves[2].wait()
    full = lax.dot_general(
        jnp.maximum(turned[1], 0), turned[2], (((1,), (1,)), ((), ())),
        preferred_element_type=F32,
    )
    state = jnp.zeros((HD, width), F32)
    for h in range(heads):
        state = jnp.where(col_head == h, full[h * HD:(h + 1) * HD, :], state)
    own_state[...] = state.astype(BF16)
    swap = remote(own_state, pair_state, x_send.at[0], x_recv.at[0], mate)
    swap.start()
    for move in q_moves[1:]:
        move.start()

    for t in range(taps):
        loads[t].wait()
        for b in range(wb.shape[0]):
            wb[b, t] = w_all[t, :, b * width:(b + 1) * width]
    w_moves = [
        remote(wb.at[far_sib_m], wsib.at[1], w_send.at[0], w_recv.at[0], sib),
        remote(wb.at[sib_m], wsib.at[0], w_send.at[1], w_recv.at[1], sib),
    ]
    for move in w_moves:
        move.start()

    moves[3].wait()
    gate[...] = jnp.transpose(turned[3])

    @pl.when(first)
    def _():
        a_own[0] = jnp.zeros((half, width), BF16)
        a_sib[0] = jnp.zeros((half, width), BF16)
        chain_in[...] = jnp.zeros((HD, width), BF16)

    @pl.when(last)
    def _():
        a_own[3] = jnp.zeros((half, width), BF16)
        a_sib[3] = jnp.zeros((half, width), BF16)

    swap.wait()
    cuts = [(0, 64), (64, HD - 64)]
    chain = [
        remote(
            chain_out.at[pl.ds(at, size), :], chain_in.at[pl.ds(at, size), :],
            c_send.at[i], c_recv.at[i], down,
        )
        for i, (at, size) in enumerate(cuts)
    ]
    for i, (at, size) in enumerate(cuts):
        @pl.when(jnp.logical_not(first))
        def _():
            chain[i].wait_recv()

        span = pl.ds(at, size)
        before = chain_in[span, :].astype(F32)
        mine = own_state[span, :].astype(F32)
        other = pair_state[span, :].astype(F32)
        low = jnp.where(x == 0, mine, other)
        chain_out[span, :] = (before + mine + other).astype(BF16)

        @pl.when(jnp.logical_not(last))
        def _():
            chain[i].start()

        own_state[span, :] = (before + low).astype(BF16)

    for j, source in enumerate((own_state, chain_out)):
        for h in range(heads):
            spread[j, h * HD:(h + 1) * HD, :] = jnp.where(col_head == h, source[...], 0)

    lanes = 128
    group = (
        lax.broadcasted_iota(jnp.int32, (width, lanes), 0) // HD
        == lax.broadcasted_iota(jnp.int32, (width, lanes), 1)
    ).astype(BF16)
    ungroup = (
        lax.broadcasted_iota(jnp.int32, (lanes, width), 1) // HD
        == lax.broadcasted_iota(jnp.int32, (lanes, width), 0)
    ).astype(BF16)

    def attend(query, prefix):
        readout = jnp.dot(jnp.maximum(query, 0), prefix, preferred_element_type=F32)
        total = jnp.dot((readout * readout).astype(BF16), group, preferred_element_type=F32)
        inverse = lax.rsqrt(total * (1.0 / HD) + 1e-06)
        coarse = inverse.astype(BF16)
        fine = (inverse - coarse.astype(F32)).astype(BF16)
        factor = jnp.dot(coarse, ungroup, preferred_element_type=F32)
        factor = factor + jnp.dot(fine, ungroup, preferred_element_type=F32)
        return (readout * factor).astype(BF16)

    def part(ref, slot, i):
        return ref.at[slot, pl.ds(pl.multiple_of(i * chunk, 16), chunk), :]

    def to_sib(slot, i):
        return remote(part(a_own, slot, i), part(a_sib, slot, i), s_send.at[slot - 1, i], s_recv.at[slot - 1, i], sib)

    def go_down(i):
        return remote(part(a_own, 2, i), part(a_own, 0, i), h_send.at[0, i], h_recv.at[0, i], down)

    def go_up(i):
        return remote(part(a_own, 1, i), part(a_own, 3, i), h_send.at[1, i], h_recv.at[1, i], up)

    def forward(j, i):
        return remote(part(a_own, 3 * j, i), part(a_sib, 3 * j, i), f_send.at[j, i], f_recv.at[j, i], sib)

    my_row = pl.multiple_of(x * shift, 16)
    for i in range(PARTS):
        span = pl.ds(i * chunk, chunk)
        mine = attend(q_ref[pl.ds(pl.multiple_of(my_row + i * chunk, 16), chunk), :], spread[x])
        a_own[1 + x, span, :] = mine
        q_moves[i].wait_recv()
        a_own[2 - x, span, :] = attend(qx[span, :], spread[1 - x])

        @pl.when(jnp.logical_not(last))
        def _():
            go_down(i).start()

        @pl.when(jnp.logical_not(first))
        def _():
            go_up(i).start()

        to_sib(1, i).start()
        to_sib(2, i).start()

    def y_move(s):
        return remote(cross.at[s], cross_in.at[s], y_send.at[s], y_recv.at[s], far)

    def b_move(i):
        return remote(back.at[i], back_in.at[i], b_send.at[i], b_recv.at[i], mate)

    def gated(total, at):
        span = pl.ds(pl.multiple_of(at, 16), chunk)
        u = gate[span, :].astype(F32)
        out_ref[span, :] = (total * (u / (1.0 + jnp.exp(-u)))).astype(BF16)

    def place(s):
        turn = s // PARTS
        return x + (1 - turn) * (1 - 2 * x), lax.rem(s, PARTS)

    def finish(s):
        j, i = place(s)
        y_move(s).wait_recv()
        total = kept[s] + cross_in[s].astype(F32)

        @pl.when(j == x)
        def _():
            gated(total, my_row + i * chunk)

        @pl.when(j != x)
        def _():
            back[i] = total.astype(BF16)
            b_move(i).start()

    w_moves[0].wait_recv()
    w_moves[1].wait_recv()

    def step(s, carry):
        j, i = place(s)
        span = pl.ds(pl.multiple_of(i * chunk, 16), chunk)

        @pl.when(s < PARTS)
        def _():
            to_sib(1, i).wait_recv()
            to_sib(2, i).wait_recv()

        def dot(a, slot, w):
            return jnp.dot(a[slot, span, :], w[...], preferred_element_type=F32)

        def inner(mine, theirs):
            acc = dot(a_own, 1, mine.at[1 - j]) + dot(a_own, 2, mine.at[2 - j])
            return acc + dot(a_sib, 1, theirs.at[1 - j]) + dot(a_sib, 2, theirs.at[2 - j])

        def outer(mine, theirs):
            return dot(a_own, 3 * j, mine.at[2 * j]) + dot(a_sib, 3 * j, theirs.at[2 * j])

        has = jnp.logical_and(p + j > 0, p + j < pairs)

        @pl.when(has)
        def _():
            remote(part(a_own, 2 - j, i), part(a_own, 3 * j, i), h_send.at[j, i], h_recv.at[j, i], sib).wait_recv()
            forward(j, i).start()

        kept[s] = inner(wb.at[far_m], wsib.at[1])

        @pl.when(has)
        def _():
            forward(j, i).wait_recv()

        cross[s] = (kept[s] + outer(wb.at[far_m], wsib.at[1])).astype(BF16)
        y_move(s).start()
        kept[s] = inner(wb.at[m], wsib.at[0]) + outer(wb.at[m], wsib.at[0])

        @pl.when(s > 0)
        def _():
            finish(s - 1)

        return carry

    steps = 2 * PARTS
    lax.fori_loop(0, steps, step, 0)
    finish(steps - 1)
    for i in range(PARTS):
        b_move(i).wait_recv()
        gated(back_in[i].astype(F32), mate_row + i * chunk)

    for move in q_moves:
        move.wait_send()
    for move in w_moves:
        move.wait_send()
    for s in range(steps):
        y_move(s).wait_send()

    for i in range(PARTS):
        to_sib(1, i).wait_send()
        to_sib(2, i).wait_send()
        b_move(i).wait_send()

        @pl.when(jnp.logical_not(last))
        def _():
            go_down(i).wait_send()
            forward(1, i).wait_send()

        @pl.when(jnp.logical_not(first))
        def _():
            go_up(i).wait_send()
            forward(0, i).wait_send()

    @pl.when(jnp.logical_not(last))
    def _():
        for move in chain:
            move.wait_send()


def shards(frames, query_act, key_act, value_act, conv_weight, gate_act):
    rows, width = query_act.shape
    taps, _, outs = conv_weight.shape
    chans = outs // width
    assert rows == TPF and frames % 2 == 0 and chans == 4
    half = -(-rows // (32 * PARTS)) * 16 * PARTS
    chunk = half // PARTS
    dma = pltpu.SemaphoreType.DMA
    vmem = pl.BlockSpec(memory_space=pltpu.VMEM)
    hbm = pl.BlockSpec(memory_space=pl.ANY)
    return pl.pallas_call(
        functools.partial(kernel, frames),
        out_shape=jax.ShapeDtypeStruct((rows, width), BF16),
        in_specs=[hbm] * 5,
        out_specs=vmem,
        scratch_shapes=[
            pltpu.VMEM((4, width, rows), BF16),
            pltpu.VMEM((rows, width), BF16),
            pltpu.VMEM((taps, width, outs), BF16),
            pltpu.VMEM((chans, taps, width, width), BF16),
            pltpu.VMEM((2, taps, width, width), BF16),
            pltpu.VMEM((rows, width), BF16),
            pltpu.VMEM((HD, width), BF16),
            pltpu.VMEM((HD, width), BF16),
            pltpu.VMEM((HD, width), BF16),
            pltpu.VMEM((HD, width), BF16),
            pltpu.VMEM((2, width, width), BF16),
            pltpu.VMEM((half, width), BF16),
            pltpu.VMEM((4, half, width), BF16),
            pltpu.VMEM((4, half, width), BF16),
            pltpu.VMEM((2 * PARTS, chunk, width), BF16),
            pltpu.VMEM((2 * PARTS, chunk, width), BF16),
            pltpu.VMEM((2 * PARTS, chunk, width), F32),
            pltpu.VMEM((PARTS, chunk, width), BF16),
            pltpu.VMEM((PARTS, chunk, width), BF16),
            dma((taps + 4,)),
            dma((2,)), dma((2,)),
            dma((1,)), dma((1,)),
            dma((2,)), dma((2,)),
            dma((PARTS,)), dma((PARTS,)),
            dma((2, PARTS)), dma((2, PARTS)),
            dma((2, PARTS)), dma((2, PARTS)),
            dma((2, PARTS)), dma((2, PARTS)),
            dma((2 * PARTS,)), dma((2 * PARTS,)),
            dma((PARTS,)), dma((PARTS,)),
        ],
        compiler_params=pltpu.CompilerParams(
            collective_id=0, has_side_effects=True, vmem_limit_bytes=56 * 1024 * 1024
        ),
    )(query_act.T, key_act.T, value_act.T, conv_weight, gate_act.T)


def solution(mesh):
    return jax.shard_map(
        functools.partial(shards, mesh.shape["frame"]),
        mesh=mesh,
        in_specs=(
            P("frame", "chan"),
            P("frame", "chan"),
            P("frame", "chan"),
            P(None, "chan", None),
            P("frame", "chan"),
        ),
        out_specs=P("frame", "chan"),
        check_vma=False,
    )
```

```python
import functools

import jax
import jax.numpy as jnp
from jax import lax
from jax.experimental import pallas as pl
from jax.experimental.pallas import tpu as pltpu
from jax.sharding import PartitionSpec as P

HD = 112
TPF = 880
PARTS = 2
PIECES = 2
F32 = jnp.float32
BF16 = jnp.bfloat16
MESH = pl.DeviceIdType.MESH


def kernel(
    frames,
    q_hbm, k_hbm, v_hbm, w_hbm, g_hbm, out_ref,
    turned, q_ref, w_all, wb, wsib, gate, own_state, pair_state, chain_in, chain_out, spread, qx,
    a_own, a_sib, cross, cross_in, kept, held, back, back_in,
    load_sem, w_send, w_recv, x_send, x_recv, c_send, c_recv, q_send, q_recv,
    s_send, s_recv, h_send, h_recv, f_send, f_recv, y_send, y_recv, b_send, b_recv,
):
    rows, width = q_ref.shape
    half = qx.shape[0]
    chunk = half // PARTS
    piece = chunk // PIECES
    shift = rows - half
    heads = width // HD
    pairs = frames // 2
    f = lax.axis_index("frame")
    m = lax.axis_index("chan")
    x = lax.rem(f, 2)
    p = f // 2
    first, last = p == 0, p == pairs - 1
    sib_m = m + 1 - 2 * lax.rem(m, 2)
    far_m = m + 2 - 4 * lax.rem(m // 2, 2)
    far_sib_m = far_m + 1 - 2 * lax.rem(far_m, 2)
    sib, far, mate = (f, sib_m), (f, far_m), (f + 1 - 2 * x, m)
    up, down = (f - 2, m), (f + 2, m)

    def remote(src, dst, send, recv, device):
        return pltpu.make_async_remote_copy(
            src_ref=src, dst_ref=dst, send_sem=send, recv_sem=recv,
            device_id=device, device_id_type=MESH,
        )

    barrier = pltpu.get_barrier_semaphore()
    for device in (sib, far, mate):
        pl.semaphore_signal(barrier, inc=1, device_id=device, device_id_type=MESH)

    @pl.when(jnp.logical_not(first))
    def _():
        pl.semaphore_signal(barrier, inc=1, device_id=up, device_id_type=MESH)

    @pl.when(jnp.logical_not(last))
    def _():
        pl.semaphore_signal(barrier, inc=1, device_id=down, device_id_type=MESH)

    taps = w_hbm.shape[0]
    moves = [
        pltpu.make_async_copy(source, turned.at[i], load_sem.at[taps + i])
        for i, source in enumerate((q_hbm, k_hbm, v_hbm, g_hbm))
    ]
    loads = [pltpu.make_async_copy(w_hbm.at[t], w_all.at[t], load_sem.at[t]) for t in range(taps)]
    for load in moves + loads:
        load.start()

    moves[0].wait()
    q_ref[...] = jnp.transpose(turned[0])
    pl.semaphore_wait(barrier, 3 + jnp.where(first, 0, 1) + jnp.where(last, 0, 1))
    mate_row = pl.multiple_of((1 - x) * shift, 16)
    q_moves = [
        remote(
            q_ref.at[pl.ds(pl.multiple_of(mate_row + i * piece, 16), piece), :],
            qx.at[pl.ds(i * piece, piece), :], q_send.at[i], q_recv.at[i], mate,
        )
        for i in range(PARTS * PIECES)
    ]
    q_moves[0].start()

    col_head = lax.broadcasted_iota(jnp.int32, (HD, width), 1) // HD
    moves[1].wait()
    moves[2].wait()
    full = lax.dot_general(
        jnp.maximum(turned[1], 0), turned[2], (((1,), (1,)), ((), ())),
        preferred_element_type=F32,
    )
    state = jnp.zeros((HD, width), F32)
    for h in range(heads):
        state = jnp.where(col_head == h, full[h * HD:(h + 1) * HD, :], state)
    own_state[...] = state.astype(BF16)
    swap = remote(own_state, pair_state, x_send.at[0], x_recv.at[0], mate)
    swap.start()
    for move in q_moves[1:]:
        move.start()

    for t in range(taps):
        loads[t].wait()
        for b in range(wb.shape[0]):
            wb[b, t] = w_all[t, :, b * width:(b + 1) * width]
    w_moves = [
        remote(wb.at[far_sib_m], wsib.at[1], w_send.at[0], w_recv.at[0], sib),
        remote(wb.at[sib_m], wsib.at[0], w_send.at[1], w_recv.at[1], sib),
    ]
    for move in w_moves:
        move.start()

    @pl.when(first)
    def _():
        a_own[0] = jnp.zeros((half, width), BF16)
        a_sib[0] = jnp.zeros((half, width), BF16)
        chain_in[...] = jnp.zeros((HD, width), BF16)

    @pl.when(last)
    def _():
        a_own[3] = jnp.zeros((half, width), BF16)
        a_sib[3] = jnp.zeros((half, width), BF16)

    swap.wait()
    cuts = [(0, 64), (64, HD - 64)]
    chain = [
        remote(
            chain_out.at[pl.ds(at, size), :], chain_in.at[pl.ds(at, size), :],
            c_send.at[i], c_recv.at[i], down,
        )
        for i, (at, size) in enumerate(cuts)
    ]
    for i, (at, size) in enumerate(cuts):
        @pl.when(jnp.logical_not(first))
        def _():
            chain[i].wait_recv()

        span = pl.ds(at, size)
        before = chain_in[span, :].astype(F32)
        mine = own_state[span, :].astype(F32)
        other = pair_state[span, :].astype(F32)
        low = jnp.where(x == 0, mine, other)
        chain_out[span, :] = (before + mine + other).astype(BF16)

        @pl.when(jnp.logical_not(last))
        def _():
            chain[i].start()

        own_state[span, :] = (before + low).astype(BF16)

    for j, source in enumerate((own_state, chain_out)):
        for h in range(heads):
            spread[j, h * HD:(h + 1) * HD, :] = jnp.where(col_head == h, source[...], 0)

    lanes = 128
    group = (
        lax.broadcasted_iota(jnp.int32, (width, lanes), 0) // HD
        == lax.broadcasted_iota(jnp.int32, (width, lanes), 1)
    ).astype(BF16)
    ungroup = (
        lax.broadcasted_iota(jnp.int32, (lanes, width), 1) // HD
        == lax.broadcasted_iota(jnp.int32, (lanes, width), 0)
    ).astype(BF16)

    def attend(query, prefix):
        readout = jnp.dot(jnp.maximum(query, 0), prefix, preferred_element_type=F32)
        total = jnp.dot((readout * readout).astype(BF16), group, preferred_element_type=F32)
        inverse = lax.rsqrt(total * (1.0 / HD) + 1e-06)
        coarse = inverse.astype(BF16)
        fine = (inverse - coarse.astype(F32)).astype(BF16)
        factor = jnp.dot(coarse, ungroup, preferred_element_type=F32)
        factor = factor + jnp.dot(fine, ungroup, preferred_element_type=F32)
        return (readout * factor).astype(BF16)

    def part(ref, slot, i):
        return ref.at[slot, pl.ds(pl.multiple_of(i * chunk, 16), chunk), :]

    def to_sib(slot, i):
        return remote(part(a_own, slot, i), part(a_sib, slot, i), s_send.at[slot - 1, i], s_recv.at[slot - 1, i], sib)

    def go_down(i):
        return remote(part(a_own, 2, i), part(a_own, 0, i), h_send.at[0, i], h_recv.at[0, i], down)

    def go_up(i):
        return remote(part(a_own, 1, i), part(a_own, 3, i), h_send.at[1, i], h_recv.at[1, i], up)

    def forward(j, i):
        return remote(part(a_own, 3 * j, i), part(a_sib, 3 * j, i), f_send.at[j, i], f_recv.at[j, i], sib)

    my_row = pl.multiple_of(x * shift, 16)
    for i in range(PARTS):
        row = pl.multiple_of(my_row + i * chunk, 16)
        a_own[1 + x, pl.ds(i * chunk, chunk), :] = attend(q_ref[pl.ds(row, chunk), :], spread[x])

        @pl.when(jnp.logical_and(x == 0, jnp.logical_not(first)))
        def _():
            go_up(i).start()

        @pl.when(jnp.logical_and(x == 1, jnp.logical_not(last)))
        def _():
            go_down(i).start()

        to_sib(1 + x, i).start()

    for i in range(PARTS):
        span = pl.ds(i * chunk, chunk)
        for move in q_moves[i * PIECES:(i + 1) * PIECES]:
            move.wait_recv()
        a_own[2 - x, span, :] = attend(qx[span, :], spread[1 - x])

        @pl.when(jnp.logical_and(x == 1, jnp.logical_not(first)))
        def _():
            go_up(i).start()

        @pl.when(jnp.logical_and(x == 0, jnp.logical_not(last)))
        def _():
            go_down(i).start()

        to_sib(2 - x, i).start()

    def y_move(s):
        return remote(cross.at[s], cross_in.at[s], y_send.at[s], y_recv.at[s], far)

    def b_move(i):
        return remote(back.at[i], back_in.at[i], b_send.at[i], b_recv.at[i], mate)

    def gated(total, at):
        span = pl.ds(pl.multiple_of(at, 16), chunk)
        u = gate[span, :].astype(F32)
        out_ref[span, :] = (total * (u / (1.0 + jnp.exp(-u)))).astype(BF16)

    def place(s):
        turn = s // PARTS
        return x + (1 - turn) * (1 - 2 * x), lax.rem(s, PARTS)

    def finish(s):
        j, i = place(s)
        y_move(s).wait_recv()
        total = kept[s] + cross_in[s].astype(F32)

        @pl.when(j == x)
        def _():
            gated(total, my_row + i * chunk)

        @pl.when(j != x)
        def _():
            back[i] = total.astype(BF16)
            b_move(i).start()

    w_moves[0].wait_recv()
    w_moves[1].wait_recv()

    def step(s, carry):
        j, i = place(s)
        span = pl.ds(pl.multiple_of(i * chunk, 16), chunk)

        @pl.when(s < PARTS)
        def _():
            to_sib(1, i).wait_recv()
            to_sib(2, i).wait_recv()

        def dot(a, slot, w):
            return jnp.dot(a[slot, span, :], w[...], preferred_element_type=F32)

        def inner(mine, theirs):
            acc = dot(a_own, 1, mine.at[1 - j]) + dot(a_own, 2, mine.at[2 - j])
            return acc + dot(a_sib, 1, theirs.at[1 - j]) + dot(a_sib, 2, theirs.at[2 - j])

        def outer(mine, theirs):
            return dot(a_own, 3 * j, mine.at[2 * j]) + dot(a_sib, 3 * j, theirs.at[2 * j])

        has = jnp.logical_and(p + j > 0, p + j < pairs)

        held[...] = inner(wb.at[far_m], wsib.at[1])

        @pl.when(has)
        def _():
            remote(part(a_own, 2 - j, i), part(a_own, 3 * j, i), h_send.at[j, i], h_recv.at[j, i], sib).wait_recv()
            forward(j, i).start()

        kept[s] = inner(wb.at[m], wsib.at[0])

        @pl.when(has)
        def _():
            forward(j, i).wait_recv()

        cross[s] = (held[...] + outer(wb.at[far_m], wsib.at[1])).astype(BF16)
        y_move(s).start()
        kept[s] += outer(wb.at[m], wsib.at[0])

        @pl.when(s == 0)
        def _():
            moves[3].wait()
            gate[...] = jnp.transpose(turned[3])

        @pl.when(s > 0)
        def _():
            finish(s - 1)

        return carry

    steps = 2 * PARTS
    lax.fori_loop(0, steps, step, 0)
    for i in range(PARTS):
        b_move(i).wait_recv()
        gated(back_in[i].astype(F32), mate_row + i * chunk)
    finish(steps - 1)

    for move in q_moves:
        move.wait_send()
    for move in w_moves:
        move.wait_send()
    for s in range(steps):
        y_move(s).wait_send()

    for i in range(PARTS):
        to_sib(1, i).wait_send()
        to_sib(2, i).wait_send()
        b_move(i).wait_send()

        @pl.when(jnp.logical_not(last))
        def _():
            go_down(i).wait_send()
            forward(1, i).wait_send()

        @pl.when(jnp.logical_not(first))
        def _():
            go_up(i).wait_send()
            forward(0, i).wait_send()

    @pl.when(jnp.logical_not(last))
    def _():
        for move in chain:
            move.wait_send()


def shards(frames, query_act, key_act, value_act, conv_weight, gate_act):
    rows, width = query_act.shape
    taps, _, outs = conv_weight.shape
    chans = outs // width
    assert rows == TPF and frames % 2 == 0 and chans == 4
    half = -(-rows // (32 * PARTS * PIECES)) * 16 * PARTS * PIECES
    chunk = half // PARTS
    dma = pltpu.SemaphoreType.DMA
    vmem = pl.BlockSpec(memory_space=pltpu.VMEM)
    hbm = pl.BlockSpec(memory_space=pl.ANY)
    return pl.pallas_call(
        functools.partial(kernel, frames),
        out_shape=jax.ShapeDtypeStruct((rows, width), BF16),
        in_specs=[hbm] * 5,
        out_specs=vmem,
        scratch_shapes=[
            pltpu.VMEM((4, width, rows), BF16),
            pltpu.VMEM((rows, width), BF16),
            pltpu.VMEM((taps, width, outs), BF16),
            pltpu.VMEM((chans, taps, width, width), BF16),
            pltpu.VMEM((2, taps, width, width), BF16),
            pltpu.VMEM((rows, width), BF16),
            pltpu.VMEM((HD, width), BF16),
            pltpu.VMEM((HD, width), BF16),
            pltpu.VMEM((HD, width), BF16),
            pltpu.VMEM((HD, width), BF16),
            pltpu.VMEM((2, width, width), BF16),
            pltpu.VMEM((half, width), BF16),
            pltpu.VMEM((4, half, width), BF16),
            pltpu.VMEM((4, half, width), BF16),
            pltpu.VMEM((2 * PARTS, chunk, width), BF16),
            pltpu.VMEM((2 * PARTS, chunk, width), BF16),
            pltpu.VMEM((2 * PARTS, chunk, width), F32),
            pltpu.VMEM((chunk, width), F32),
            pltpu.VMEM((PARTS, chunk, width), BF16),
            pltpu.VMEM((PARTS, chunk, width), BF16),
            dma((taps + 4,)),
            dma((2,)), dma((2,)),
            dma((1,)), dma((1,)),
            dma((2,)), dma((2,)),
            dma((PARTS * PIECES,)), dma((PARTS * PIECES,)),
            dma((2, PARTS)), dma((2, PARTS)),
            dma((2, PARTS)), dma((2, PARTS)),
            dma((2, PARTS)), dma((2, PARTS)),
            dma((2 * PARTS,)), dma((2 * PARTS,)),
            dma((PARTS,)), dma((PARTS,)),
        ],
        compiler_params=pltpu.CompilerParams(
            collective_id=0, has_side_effects=True, vmem_limit_bytes=56 * 1024 * 1024
        ),
    )(query_act.T, key_act.T, value_act.T, conv_weight, gate_act.T)


def solution(mesh):
    return jax.shard_map(
        functools.partial(shards, mesh.shape["frame"]),
        mesh=mesh,
        in_specs=(
            P("frame", "chan"),
            P("frame", "chan"),
            P("frame", "chan"),
            P(None, "chan", None),
            P("frame", "chan"),
        ),
        out_specs=P("frame", "chan"),
        check_vma=False,
    )
```

```python
import functools

import jax
import jax.numpy as jnp
from jax import lax
from jax.experimental import pallas as pl
from jax.experimental.pallas import tpu as pltpu
from jax.sharding import PartitionSpec as P

HD = 112
TPF = 880
PARTS = 2
PIECES = 2
F32 = jnp.float32
BF16 = jnp.bfloat16
MESH = pl.DeviceIdType.MESH


def kernel(
    frames,
    q_hbm, k_hbm, v_hbm, w_hbm, g_hbm, out_ref,
    turned, q_ref, w_all, wb, wsib, gate, own_state, pair_state, chain_in, chain_out, spread, qx,
    a_own, a_sib, cross, cross_in, kept, held, back, back_in,
    load_sem, w_send, w_recv, x_send, x_recv, c_send, c_recv, q_send, q_recv,
    s_send, s_recv, h_send, h_recv, f_send, f_recv, y_send, y_recv, b_send, b_recv,
):
    rows, width = q_ref.shape
    half = qx.shape[0]
    chunk = half // PARTS
    piece = chunk // PIECES
    shift = rows - half
    heads = width // HD
    pairs = frames // 2
    f = lax.axis_index("frame")
    m = lax.axis_index("chan")
    x = lax.rem(f, 2)
    p = f // 2
    first, last = p == 0, p == pairs - 1
    sib_m = m + 1 - 2 * lax.rem(m, 2)
    far_m = m + 2 - 4 * lax.rem(m // 2, 2)
    far_sib_m = far_m + 1 - 2 * lax.rem(far_m, 2)
    sib, far, mate = (f, sib_m), (f, far_m), (f + 1 - 2 * x, m)
    up, down = (f - 2, m), (f + 2, m)

    def remote(src, dst, send, recv, device):
        return pltpu.make_async_remote_copy(
            src_ref=src, dst_ref=dst, send_sem=send, recv_sem=recv,
            device_id=device, device_id_type=MESH,
        )

    barrier = pltpu.get_barrier_semaphore()
    for device in (sib, far, mate):
        pl.semaphore_signal(barrier, inc=1, device_id=device, device_id_type=MESH)

    @pl.when(jnp.logical_not(first))
    def _():
        pl.semaphore_signal(barrier, inc=1, device_id=up, device_id_type=MESH)

    @pl.when(jnp.logical_not(last))
    def _():
        pl.semaphore_signal(barrier, inc=1, device_id=down, device_id_type=MESH)

    taps = w_hbm.shape[0]
    moves = [
        pltpu.make_async_copy(source, turned.at[i], load_sem.at[taps + i])
        for i, source in enumerate((q_hbm, k_hbm, v_hbm, g_hbm))
    ]
    loads = [pltpu.make_async_copy(w_hbm.at[t], w_all.at[t], load_sem.at[t]) for t in range(taps)]
    for load in moves + loads:
        load.start()

    moves[0].wait()
    q_ref[...] = jnp.transpose(turned[0])
    pl.semaphore_wait(barrier, 3 + jnp.where(first, 0, 1) + jnp.where(last, 0, 1))
    mate_row = pl.multiple_of((1 - x) * shift, 16)
    q_moves = [
        remote(
            q_ref.at[pl.ds(pl.multiple_of(mate_row + i * piece, 16), piece), :],
            qx.at[pl.ds(i * piece, piece), :], q_send.at[i], q_recv.at[i], mate,
        )
        for i in range(PARTS * PIECES)
    ]
    q_moves[0].start()

    col_head = lax.broadcasted_iota(jnp.int32, (HD, width), 1) // HD
    moves[1].wait()
    moves[2].wait()
    full = lax.dot_general(
        jnp.maximum(turned[1], 0), turned[2], (((1,), (1,)), ((), ())),
        preferred_element_type=F32,
    )
    state = jnp.zeros((HD, width), F32)
    for h in range(heads):
        state = jnp.where(col_head == h, full[h * HD:(h + 1) * HD, :], state)
    own_state[...] = state.astype(BF16)
    swap = remote(own_state, pair_state, x_send.at[0], x_recv.at[0], mate)
    swap.start()
    for move in q_moves[1:]:
        move.start()

    for t in range(taps):
        loads[t].wait()
        for b in range(wb.shape[0]):
            wb[b, t] = w_all[t, :, b * width:(b + 1) * width]
    w_moves = [
        remote(wb.at[far_sib_m], wsib.at[1], w_send.at[0], w_recv.at[0], sib),
        remote(wb.at[sib_m], wsib.at[0], w_send.at[1], w_recv.at[1], sib),
    ]
    for move in w_moves:
        move.start()

    @pl.when(first)
    def _():
        a_own[0] = jnp.zeros((half, width), BF16)
        a_sib[0] = jnp.zeros((half, width), BF16)
        chain_in[...] = jnp.zeros((HD, width), BF16)

    @pl.when(last)
    def _():
        a_own[3] = jnp.zeros((half, width), BF16)
        a_sib[3] = jnp.zeros((half, width), BF16)

    swap.wait()
    cuts = [(0, 64), (64, HD - 64)]
    chain = [
        remote(
            chain_out.at[pl.ds(at, size), :], chain_in.at[pl.ds(at, size), :],
            c_send.at[i], c_recv.at[i], down,
        )
        for i, (at, size) in enumerate(cuts)
    ]
    for i, (at, size) in enumerate(cuts):
        @pl.when(jnp.logical_not(first))
        def _():
            chain[i].wait_recv()

        span = pl.ds(at, size)
        before = chain_in[span, :].astype(F32)
        mine = own_state[span, :].astype(F32)
        other = pair_state[span, :].astype(F32)
        low = jnp.where(x == 0, mine, other)
        chain_out[span, :] = (before + mine + other).astype(BF16)

        @pl.when(jnp.logical_not(last))
        def _():
            chain[i].start()

        own_state[span, :] = (before + low).astype(BF16)

    for j, source in enumerate((own_state, chain_out)):
        for h in range(heads):
            spread[j, h * HD:(h + 1) * HD, :] = jnp.where(col_head == h, source[...], 0)

    lanes = 128
    group = (
        lax.broadcasted_iota(jnp.int32, (width, lanes), 0) // HD
        == lax.broadcasted_iota(jnp.int32, (width, lanes), 1)
    ).astype(BF16)
    ungroup = (
        lax.broadcasted_iota(jnp.int32, (lanes, width), 1) // HD
        == lax.broadcasted_iota(jnp.int32, (lanes, width), 0)
    ).astype(BF16)

    def attend(query, prefix):
        readout = jnp.dot(jnp.maximum(query, 0), prefix, preferred_element_type=F32)
        total = jnp.dot((readout * readout).astype(BF16), group, preferred_element_type=F32)
        inverse = lax.rsqrt(total * (1.0 / HD) + 1e-06)
        coarse = inverse.astype(BF16)
        fine = (inverse - coarse.astype(F32)).astype(BF16)
        factor = jnp.dot(coarse, ungroup, preferred_element_type=F32)
        factor = factor + jnp.dot(fine, ungroup, preferred_element_type=F32)
        return (readout * factor).astype(BF16)

    def part(ref, slot, i):
        return ref.at[slot, pl.ds(pl.multiple_of(i * chunk, 16), chunk), :]

    def to_sib(slot, i):
        return remote(part(a_own, slot, i), part(a_sib, slot, i), s_send.at[slot - 1, i], s_recv.at[slot - 1, i], sib)

    def go_down(i):
        return remote(part(a_own, 2, i), part(a_own, 0, i), h_send.at[0, i], h_recv.at[0, i], down)

    def go_up(i):
        return remote(part(a_own, 1, i), part(a_own, 3, i), h_send.at[1, i], h_recv.at[1, i], up)

    def forward(j, i):
        return remote(part(a_own, 3 * j, i), part(a_sib, 3 * j, i), f_send.at[j, i], f_recv.at[j, i], sib)

    def halo_out(i):
        @pl.when(jnp.logical_and(x == 0, jnp.logical_not(first)))
        def _():
            go_up(i).start()

        @pl.when(jnp.logical_and(x == 1, jnp.logical_not(last)))
        def _():
            go_down(i).start()

    my_row = pl.multiple_of(x * shift, 16)
    for i in range(PARTS):
        row = pl.multiple_of(my_row + i * chunk, 16)
        a_own[1 + x, pl.ds(i * chunk, chunk), :] = attend(q_ref[pl.ds(row, chunk), :], spread[x])

        if i == 0:
            halo_out(0)
        to_sib(1 + x, i).start()

    for i in range(PARTS):
        span = pl.ds(i * chunk, chunk)
        for move in q_moves[i * PIECES:(i + 1) * PIECES]:
            move.wait_recv()
        a_own[2 - x, span, :] = attend(qx[span, :], spread[1 - x])

        @pl.when(jnp.logical_and(x == 1, jnp.logical_not(first)))
        def _():
            go_up(i).start()

        @pl.when(jnp.logical_and(x == 0, jnp.logical_not(last)))
        def _():
            go_down(i).start()

        to_sib(2 - x, i).start()

    def y_move(s):
        return remote(cross.at[s], cross_in.at[s], y_send.at[s], y_recv.at[s], far)

    def b_move(i):
        return remote(back.at[i], back_in.at[i], b_send.at[i], b_recv.at[i], mate)

    def gated(total, at):
        span = pl.ds(pl.multiple_of(at, 16), chunk)
        u = gate[span, :].astype(F32)
        out_ref[span, :] = (total * (u / (1.0 + jnp.exp(-u)))).astype(BF16)

    def place(s):
        turn = s // PARTS
        return x + (1 - turn) * (1 - 2 * x), lax.rem(s, PARTS)

    def finish(s):
        j, i = place(s)
        y_move(s).wait_recv()
        total = kept[s] + cross_in[s].astype(F32)

        @pl.when(j == x)
        def _():
            gated(total, my_row + i * chunk)

        @pl.when(j != x)
        def _():
            back[i] = total.astype(BF16)
            b_move(i).start()

    w_moves[0].wait_recv()
    w_moves[1].wait_recv()

    def step(s, carry):
        j, i = place(s)
        span = pl.ds(pl.multiple_of(i * chunk, 16), chunk)

        @pl.when(s < PARTS)
        def _():
            to_sib(1, i).wait_recv()
            to_sib(2, i).wait_recv()

        def dot(a, slot, w):
            return jnp.dot(a[slot, span, :], w[...], preferred_element_type=F32)

        def inner(mine, theirs):
            acc = dot(a_own, 1, mine.at[1 - j]) + dot(a_own, 2, mine.at[2 - j])
            return acc + dot(a_sib, 1, theirs.at[1 - j]) + dot(a_sib, 2, theirs.at[2 - j])

        def outer(mine, theirs):
            return dot(a_own, 3 * j, mine.at[2 * j]) + dot(a_sib, 3 * j, theirs.at[2 * j])

        has = jnp.logical_and(p + j > 0, p + j < pairs)

        held[...] = inner(wb.at[far_m], wsib.at[1])

        @pl.when(has)
        def _():
            remote(part(a_own, 2 - j, i), part(a_own, 3 * j, i), h_send.at[j, i], h_recv.at[j, i], sib).wait_recv()
            forward(j, i).start()

        @pl.when(s == 0)
        def _():
            for later in range(1, PARTS):
                halo_out(later)

        kept[s] = inner(wb.at[m], wsib.at[0])

        @pl.when(has)
        def _():
            forward(j, i).wait_recv()

        cross[s] = (held[...] + outer(wb.at[far_m], wsib.at[1])).astype(BF16)
        y_move(s).start()
        kept[s] += outer(wb.at[m], wsib.at[0])

        @pl.when(s == 0)
        def _():
            moves[3].wait()
            gate[...] = jnp.transpose(turned[3])

        @pl.when(s > 0)
        def _():
            finish(s - 1)

        return carry

    steps = 2 * PARTS
    lax.fori_loop(0, steps, step, 0)
    for i in range(PARTS):
        b_move(i).wait_recv()
        gated(back_in[i].astype(F32), mate_row + i * chunk)
    finish(steps - 1)

    for move in q_moves:
        move.wait_send()
    for move in w_moves:
        move.wait_send()
    for s in range(steps):
        y_move(s).wait_send()

    for i in range(PARTS):
        to_sib(1, i).wait_send()
        to_sib(2, i).wait_send()
        b_move(i).wait_send()

        @pl.when(jnp.logical_not(last))
        def _():
            go_down(i).wait_send()
            forward(1, i).wait_send()

        @pl.when(jnp.logical_not(first))
        def _():
            go_up(i).wait_send()
            forward(0, i).wait_send()

    @pl.when(jnp.logical_not(last))
    def _():
        for move in chain:
            move.wait_send()


def shards(frames, query_act, key_act, value_act, conv_weight, gate_act):
    rows, width = query_act.shape
    taps, _, outs = conv_weight.shape
    chans = outs // width
    assert rows == TPF and frames % 2 == 0 and chans == 4
    half = -(-rows // (32 * PARTS * PIECES)) * 16 * PARTS * PIECES
    chunk = half // PARTS
    dma = pltpu.SemaphoreType.DMA
    vmem = pl.BlockSpec(memory_space=pltpu.VMEM)
    hbm = pl.BlockSpec(memory_space=pl.ANY)
    return pl.pallas_call(
        functools.partial(kernel, frames),
        out_shape=jax.ShapeDtypeStruct((rows, width), BF16),
        in_specs=[hbm] * 5,
        out_specs=vmem,
        scratch_shapes=[
            pltpu.VMEM((4, width, rows), BF16),
            pltpu.VMEM((rows, width), BF16),
            pltpu.VMEM((taps, width, outs), BF16),
            pltpu.VMEM((chans, taps, width, width), BF16),
            pltpu.VMEM((2, taps, width, width), BF16),
            pltpu.VMEM((rows, width), BF16),
            pltpu.VMEM((HD, width), BF16),
            pltpu.VMEM((HD, width), BF16),
            pltpu.VMEM((HD, width), BF16),
            pltpu.VMEM((HD, width), BF16),
            pltpu.VMEM((2, width, width), BF16),
            pltpu.VMEM((half, width), BF16),
            pltpu.VMEM((4, half, width), BF16),
            pltpu.VMEM((4, half, width), BF16),
            pltpu.VMEM((2 * PARTS, chunk, width), BF16),
            pltpu.VMEM((2 * PARTS, chunk, width), BF16),
            pltpu.VMEM((2 * PARTS, chunk, width), F32),
            pltpu.VMEM((chunk, width), F32),
            pltpu.VMEM((PARTS, chunk, width), BF16),
            pltpu.VMEM((PARTS, chunk, width), BF16),
            dma((taps + 4,)),
            dma((2,)), dma((2,)),
            dma((1,)), dma((1,)),
            dma((2,)), dma((2,)),
            dma((PARTS * PIECES,)), dma((PARTS * PIECES,)),
            dma((2, PARTS)), dma((2, PARTS)),
            dma((2, PARTS)), dma((2, PARTS)),
            dma((2, PARTS)), dma((2, PARTS)),
            dma((2 * PARTS,)), dma((2 * PARTS,)),
            dma((PARTS,)), dma((PARTS,)),
        ],
        compiler_params=pltpu.CompilerParams(
            collective_id=0, has_side_effects=True, vmem_limit_bytes=56 * 1024 * 1024
        ),
    )(query_act.T, key_act.T, value_act.T, conv_weight, gate_act.T)


def solution(mesh):
    return jax.shard_map(
        functools.partial(shards, mesh.shape["frame"]),
        mesh=mesh,
        in_specs=(
            P("frame", "chan"),
            P("frame", "chan"),
            P("frame", "chan"),
            P(None, "chan", None),
            P("frame", "chan"),
        ),
        out_specs=P("frame", "chan"),
        check_vma=False,
    )
```
